32 devices in a mesh: strings: 2 (over y), ka: 4 (over x, core), coef: 4 (over z).
Axes of the slice: x: 2, y: 2, z: 4, core: 2. Of those that a mesh axis runs over, the one named last changes fastest.
Arguments:
- wavefunctions: float32 [8, 49152, 384], P(('strings', 'ka'), 'coef'), parts along dimension 0, may hold values from -8 to 8
Outputs:
- transported: float32 [8, 49152, 384], P(('strings', 'ka'), 'coef'), parts along dimension 0
The draws below stay inside these ranges and needn't reach their ends.
There are 2 independent parts, one for each index of `strings`. The reference program is written for one: setup_inputs(seed, part) draws one part's arguments, and reference() takes and returns one part's arrays. A program takes and returns all parts, laid end to end along the dimension named above; each array names one. Nothing has to cross between parts.
All inputs are finite; a program needn't handle non-finite values.
Results may differ from the reference program's by a relative error of at most 0.0003.
Values sent between devices are 32-bit elements; how exact they have to be, the bound alone decides.
A program may use at most 128 MiB of HBM per device.

```python
import jax
import jax.numpy as jnp
from jax import lax

G = 49152
NB = 384
NS_ITERS = 3
K = 4


def draw_wavefunctions(key, part):
    key_base, key_frames = jax.random.split(jax.random.fold_in(key, 11), 2)
    base = jax.random.normal(key_base, (G, NB), jnp.float32)
    identity = jnp.eye(NB, dtype=jnp.float32)

    def one_point(index_k):
        subkey = jax.random.fold_in(key_frames, index_k)
        key_skew, key_mix, key_noise = jax.random.split(subkey, 3)
        skew_raw = jax.random.normal(key_skew, (NB, NB), jnp.float32) * (0.6 / jnp.sqrt(NB * 1.0))
        skew = skew_raw - skew_raw.T
        rotation = jnp.linalg.solve(identity - skew, identity + skew)
        mixing = identity + 0.1 * jax.random.normal(key_mix, (NB, NB), jnp.float32) / jnp.sqrt(NB * 1.0)
        frame = jnp.dot(rotation, mixing, precision=lax.Precision.HIGHEST)
        noise = 0.3 * jax.random.normal(key_noise, (G, NB), jnp.float32)
        values = jnp.dot(base, frame, precision=lax.Precision.HIGHEST) + noise
        return jnp.clip(values, -8.0, 8.0)
    return lax.map(one_point, jnp.arange(K, dtype=jnp.int32))


def setup_inputs(seed: int = 0, part: int = 0) -> dict:
    key_of = jax.random.split(jax.random.key(seed), 2)
    part_keys = jax.random.split(jax.random.fold_in(key_of[1], part), 2)
    wavefunctions = draw_wavefunctions(jax.random.fold_in(jax.random.fold_in(key_of[1], part), 71), part)
    return dict(wavefunctions=wavefunctions)


def polar_factor(matrix):
    norm_scale = jnp.sqrt(NB * jnp.mean(matrix * matrix) + 1e-06)
    iterate = matrix / norm_scale
    for iteration in range(NS_ITERS):
        gram_matrix = jnp.dot(iterate.T, iterate, precision=lax.Precision.HIGHEST)
        iterate = 1.5 * iterate - 0.5 * jnp.dot(iterate, gram_matrix, precision=lax.Precision.HIGHEST)
    return iterate

def reference(wavefunctions):
    indices = jnp.arange(K, dtype=jnp.int32)

    def unitary_at(index_k):
        before_k = jnp.where(index_k == 0, K - 1, index_k - 1).astype(jnp.int32)
        earlier = lax.dynamic_index_in_dim(wavefunctions, before_k, 0, keepdims=False)
        current = lax.dynamic_index_in_dim(wavefunctions, index_k, 0, keepdims=False)
        margin = jnp.dot(earlier.T, current, precision=lax.Precision.HIGHEST) / G
        return polar_factor(margin)
    unitaries = lax.map(unitary_at, indices)

    def advance(product, unitary):
        product = jnp.dot(product, unitary, precision=lax.Precision.HIGHEST)
        return (product, product)
    start = jnp.eye(NB, dtype=jnp.float32)
    last_product, products = lax.scan(advance, start, unitaries)

    def rotate(index_k):
        current = lax.dynamic_index_in_dim(wavefunctions, index_k, 0, keepdims=False)
        product = lax.dynamic_index_in_dim(products, index_k, 0, keepdims=False)
        return jnp.dot(current, product.T, precision=lax.Precision.HIGHEST)
    return lax.map(rotate, indices)
```

```python
import functools

import jax
import jax.numpy as jnp
from jax import lax
from jax.experimental import pallas as pl
from jax.experimental.pallas import tpu as pltpu
from jax.sharding import PartitionSpec as P

G = 49152
NB = 384
NS_ITERS = 3
MESH = pl.DeviceIdType.MESH
MIB = 1024 * 1024


def split(x):
    high = x.astype(jnp.bfloat16)
    low = (x - high.astype(jnp.float32)).astype(jnp.bfloat16)
    return high, low


def dot3(a, b, dims):
    a_high, a_low = split(a)
    b_high, b_low = split(b)
    dot = functools.partial(
        lax.dot_general, dimension_numbers=(dims, ((), ())), preferred_element_type=jnp.float32
    )
    return dot(a_high, b_high) + (dot(a_low, b_high) + dot(a_high, b_low))


def matmul(a, b):
    return dot3(a, b, ((1,), (0,)))


def polar(margin):
    scale = jnp.sqrt(NB * jnp.mean(margin * margin, keepdims=True) + 1e-06)
    iterate = margin / scale
    for _ in range(NS_ITERS):
        gram = dot3(iterate, iterate, ((0,), (0,)))
        iterate = 1.5 * iterate - 0.5 * matmul(iterate, gram)
    return iterate


def unitary_kernel(n, part_ref, unitary_ref, arrived, full, send1, recv1, send2, recv2):
    me = lax.axis_index("coef")
    rows = part_ref.shape[0] // n
    peers = [lax.rem(me + d, n) for d in range(n)]

    def own(device):
        return pl.ds(pl.multiple_of(device * rows, 8), rows)

    barrier = pltpu.get_barrier_semaphore()
    for d in range(1, n):
        pl.semaphore_signal(barrier, inc=1, device_id={"coef": peers[d]}, device_id_type=MESH)
    pl.semaphore_wait(barrier, n - 1)

    scatter, gather = [], []
    for d in range(1, n):
        copy = pltpu.make_async_remote_copy(
            src_ref=part_ref.at[own(peers[d])], dst_ref=arrived.at[d],
            send_sem=send1.at[d], recv_sem=recv1.at[d],
            device_id={"coef": peers[d]}, device_id_type=MESH,
        )
        copy.start()
        scatter.append(copy)
    total = part_ref[own(me), :]
    for d in range(1, n):
        scatter[d - 1].wait_recv()
        total += arrived[d]
    full[own(me), :] = total
    for d in range(1, n):
        copy = pltpu.make_async_remote_copy(
            src_ref=full.at[own(me)], dst_ref=full.at[own(me)],
            send_sem=send2.at[d], recv_sem=recv2.at[d],
            device_id={"coef": peers[d]}, device_id_type=MESH,
        )
        copy.start()
        gather.append(copy)
    for d in range(1, n):
        gather[d - 1].wait_recv()
    for copy in scatter + gather:
        copy.wait_send()
    unitary_ref[...] = polar(full[...] / G)


def unitary_of(part, n):
    rows, columns = part.shape
    return pl.pallas_call(
        functools.partial(unitary_kernel, n),
        out_shape=jax.ShapeDtypeStruct(part.shape, jnp.float32),
        in_specs=[pl.BlockSpec(memory_space=pltpu.VMEM)],
        out_specs=pl.BlockSpec(memory_space=pltpu.VMEM),
        scratch_shapes=[
            pltpu.VMEM((n, rows // n, columns), jnp.float32),
            pltpu.VMEM((rows, columns), jnp.float32),
        ] + [pltpu.SemaphoreType.DMA((n,))] * 4,
        compiler_params=pltpu.CompilerParams(
            collective_id=0, has_side_effects=True, vmem_limit_bytes=24 * MIB
        ),
    )(part)


def transport_kernel(psi_ref, product_ref, out_ref, weights):
    @pl.when(pl.program_id(0) == 0)
    def _():
        high, low = split(product_ref[...].T)
        weights[...] = jnp.concatenate([high, high, low], axis=0)

    high, low = split(psi_ref[...])
    out_ref[...] = jnp.dot(
        jnp.concatenate([high, low, high], axis=1), weights[...],
        preferred_element_type=jnp.float32,
    )


def transport(psi, product):
    rows, columns = psi.shape
    block = 1024 if rows % 1024 == 0 else rows
    return pl.pallas_call(
        transport_kernel,
        grid=(rows // block,),
        out_shape=jax.ShapeDtypeStruct(psi.shape, jnp.float32),
        in_specs=[
            pl.BlockSpec((block, columns), lambda i: (i, 0)),
            pl.BlockSpec((columns, columns), lambda i: (0, 0)),
        ],
        out_specs=pl.BlockSpec((block, columns), lambda i: (i, 0)),
        scratch_shapes=[pltpu.VMEM((3 * columns, columns), jnp.bfloat16)],
        compiler_params=pltpu.CompilerParams(vmem_limit_bytes=32 * MIB),
    )(psi, product)


def on_device(wavefunctions):
    psi = wavefunctions[0]
    n_ka, n_coef = lax.axis_size("ka"), lax.axis_size("coef")
    rows = psi.shape[0]
    chunks = 8
    size = rows // chunks
    route = [((i - 1) % n_ka, i) for i in range(n_ka)]
    part = None
    blocks = [psi[c * size:(c + 1) * size] for c in range(chunks)]
    carried = [lax.ppermute(block, "ka", route) for block in blocks]
    for earlier, block in zip(carried, blocks):
        term = jnp.dot(earlier.T, block, precision=lax.Precision.HIGH)
        part = term if part is None else part + term
    if NB % (8 * n_coef) == 0:
        unitary = unitary_of(part, n_coef)
    else:
        unitary = polar(lax.psum(part, "coef") / G)
    unitaries = lax.all_gather(unitary, "ka", axis=0)
    position = lax.axis_index("ka")
    product = lax.fori_loop(
        1, position + 1,
        lambda k, total: jnp.dot(total, unitaries[k], precision=lax.Precision.HIGHEST),
        unitaries[0],
    )
    return transport(psi, product)[None]


def solution(mesh):
    placed = (P(("strings", "ka"), "coef", None),)
    return jax.shard_map(
        on_device,
        mesh=mesh,
        in_specs=placed,
        out_specs=P(("strings", "ka"), "coef", None),
        check_vma=False,
    )
```

```python
import functools

import jax
import jax.numpy as jnp
from jax import lax
from jax.experimental import pallas as pl
from jax.experimental.pallas import tpu as pltpu
from jax.sharding import PartitionSpec as P

G = 49152
NB = 384
NS_ITERS = 3
MESH = pl.DeviceIdType.MESH
MIB = 1024 * 1024


def split(x):
    high = x.astype(jnp.bfloat16)
    low = (x - high.astype(jnp.float32)).astype(jnp.bfloat16)
    return high, low


def dot3(a, b, dims):
    a_high, a_low = split(a)
    b_high, b_low = split(b)
    dot = functools.partial(
        lax.dot_general, dimension_numbers=(dims, ((), ())), preferred_element_type=jnp.float32
    )
    return dot(a_high, b_high) + (dot(a_low, b_high) + dot(a_high, b_low))


def matmul(a, b):
    return dot3(a, b, ((1,), (0,)))


def polar(margin):
    scale = jnp.sqrt(NB * jnp.mean(margin * margin, keepdims=True) + 1e-06)
    iterate = margin / scale
    for _ in range(NS_ITERS):
        gram = dot3(iterate, iterate, ((0,), (0,)))
        iterate = 1.5 * iterate - 0.5 * matmul(iterate, gram)
    return iterate


def product_kernel(
    n, n_coef, chunks, psi_ref, product_ref,
    carried, own, part, arrived, full, unitary, theirs, pair, earlier,
    load_sem, ring_send, ring_recv, send1, recv1, send2, recv2,
    swap_send, swap_recv, hop_send, hop_recv, pass_send, pass_recv,
):
    me, my_coef = lax.axis_index("ka"), lax.axis_index("coef")
    core, chip = lax.rem(me, 2), me // 2
    pairs = n // 2
    partner = me + 1 - 2 * core
    right = lax.rem(me + 1, n)
    size = psi_ref.shape[0] // chunks
    rows = NB // n_coef
    half = NB // 2
    peers = [lax.rem(my_coef + d, n_coef) for d in range(n_coef)]

    barrier = pltpu.get_barrier_semaphore()
    for d in range(1, n):
        pl.semaphore_signal(
            barrier, inc=1, device_id={"ka": lax.rem(me + d, n)}, device_id_type=MESH
        )
    for d in range(1, n_coef):
        pl.semaphore_signal(barrier, inc=1, device_id={"coef": peers[d]}, device_id_type=MESH)
    pl.semaphore_wait(barrier, n - 1 + n_coef - 1)

    def chunk(c):
        return pl.ds(pl.multiple_of(c * size, 8), size)

    def ring(c):
        return pltpu.make_async_remote_copy(
            src_ref=psi_ref.at[chunk(c)], dst_ref=carried.at[chunk(c)],
            send_sem=ring_send.at[c], recv_sem=ring_recv.at[c],
            device_id={"ka": right}, device_id_type=MESH,
        )

    def load(c):
        return pltpu.make_async_copy(psi_ref.at[chunk(c)], own.at[chunk(c)], load_sem.at[c])

    @pl.loop(0, chunks)
    def _(c):
        ring(c).start()
        load(c).start()

    part[...] = jnp.zeros_like(part)

    @pl.loop(0, chunks)
    def _(c):
        load(c).wait()
        ring(c).wait_recv()
        part[...] += dot3(carried[chunk(c), :], own[chunk(c), :], ((0,), (0,)))

    def own_rows(device):
        return pl.ds(pl.multiple_of(device * rows, 8), rows)

    def send(src, dst, send_sem, recv_sem, device):
        copy = pltpu.make_async_remote_copy(
            src_ref=src, dst_ref=dst, send_sem=send_sem, recv_sem=recv_sem,
            device_id=device, device_id_type=MESH,
        )
        copy.start()
        return copy

    scatter = [
        send(part.at[own_rows(peers[d])], arrived.at[d], send1.at[d], recv1.at[d],
             {"coef": peers[d]})
        for d in range(1, n_coef)
    ]
    total = part[own_rows(my_coef), :]
    for d in range(1, n_coef):
        scatter[d - 1].wait_recv()
        total += arrived[d]
    full[own_rows(my_coef), :] = total
    gather = [
        send(full.at[own_rows(my_coef)], full.at[own_rows(my_coef)], send2.at[d], recv2.at[d],
             {"coef": peers[d]})
        for d in range(1, n_coef)
    ]
    for copy in gather:
        copy.wait_recv()
    unitary[...] = polar(full[...] / G)

    swap = send(unitary, theirs, swap_send, swap_recv, {"ka": partner})
    swap.wait_recv()

    @pl.when(core == 0)
    def _():
        pair[...] = matmul(unitary[...], theirs[...])
        product_ref[...] = unitary[...]

    @pl.when(core == 1)
    def _():
        pair[...] = matmul(theirs[...], unitary[...])
        product_ref[...] = pair[...]

    mine = pl.ds(pl.multiple_of(core * half, 8), half)
    hops = [
        send(pair.at[mine], earlier.at[d, mine], hop_send.at[d], hop_recv.at[d],
             {"ka": 2 * lax.rem(chip + d, pairs) + core})
        for d in range(1, pairs)
    ]
    passes = []
    for d in range(1, pairs):
        hops[d - 1].wait_recv()
        passes.append(
            send(earlier.at[d, mine], earlier.at[d, mine], pass_send.at[d], pass_recv.at[d],
                 {"ka": partner})
        )
    for d in range(1, pairs):
        passes[d - 1].wait_recv()

        @pl.when(chip >= d)
        def _():
            product_ref[...] = matmul(earlier[d], product_ref[...])

    for copy in scatter + gather + [swap] + hops + passes:
        copy.wait_send()

    @pl.loop(0, chunks)
    def _(c):
        ring(c).wait_send()


def ordered_product(psi, n, n_coef, chunks):
    square = pltpu.VMEM((NB, NB), jnp.float32)
    dma = pltpu.SemaphoreType.DMA
    return pl.pallas_call(
        functools.partial(product_kernel, n, n_coef, chunks),
        out_shape=jax.ShapeDtypeStruct((NB, NB), jnp.float32),
        in_specs=[pl.BlockSpec(memory_space=pl.ANY)],
        out_specs=pl.BlockSpec(memory_space=pltpu.VMEM),
        scratch_shapes=[
            pltpu.VMEM(psi.shape, jnp.float32),
            pltpu.VMEM(psi.shape, jnp.float32),
            square,
            pltpu.VMEM((n_coef, NB // n_coef, NB), jnp.float32),
            square, square, square, square,
            pltpu.VMEM((n // 2, NB, NB), jnp.float32),
        ]
        + [dma((chunks,))] * 3
        + [dma((n_coef,))] * 4
        + [dma] * 2
        + [dma((n // 2,))] * 4,
        compiler_params=pltpu.CompilerParams(
            collective_id=0, has_side_effects=True, vmem_limit_bytes=58 * MIB
        ),
    )(psi)


def transport_kernel(psi_ref, product_ref, out_ref, weights):
    @pl.when(pl.program_id(0) == 0)
    def _():
        high, low = split(product_ref[...].T)
        weights[...] = jnp.concatenate([high, high, low], axis=0)

    high, low = split(psi_ref[...])
    out_ref[...] = jnp.dot(
        jnp.concatenate([high, low, high], axis=1), weights[...],
        preferred_element_type=jnp.float32,
    )


def transport(psi, product):
    rows, columns = psi.shape
    block = 1024 if rows % 1024 == 0 else rows
    return pl.pallas_call(
        transport_kernel,
        grid=(rows // block,),
        out_shape=jax.ShapeDtypeStruct(psi.shape, jnp.float32),
        in_specs=[
            pl.BlockSpec((block, columns), lambda i: (i, 0)),
            pl.BlockSpec((columns, columns), lambda i: (0, 0)),
        ],
        out_specs=pl.BlockSpec((block, columns), lambda i: (i, 0)),
        scratch_shapes=[pltpu.VMEM((3 * columns, columns), jnp.bfloat16)],
        compiler_params=pltpu.CompilerParams(vmem_limit_bytes=56 * MIB),
    )(psi, product)


def on_device(wavefunctions):
    psi = wavefunctions[0]
    n_ka, n_coef = lax.axis_size("ka"), lax.axis_size("coef")
    chunks = 16
    if n_ka % 2 == 0 and NB % (8 * n_coef) == 0 and psi.shape[0] % (8 * chunks) == 0:
        return transport(psi, ordered_product(psi, n_ka, n_coef, chunks))[None]
    route = [((i - 1) % n_ka, i) for i in range(n_ka)]
    carried = lax.ppermute(psi, "ka", route)
    part = jnp.dot(carried.T, psi, precision=lax.Precision.HIGH)
    unitary = polar(lax.psum(part, "coef") / G)
    unitaries = lax.all_gather(unitary, "ka", axis=0)
    product = lax.fori_loop(
        1, lax.axis_index("ka") + 1,
        lambda k, total: jnp.dot(total, unitaries[k], precision=lax.Precision.HIGHEST),
        unitaries[0],
    )
    return transport(psi, product)[None]


def solution(mesh):
    placed = (P(("strings", "ka"), "coef", None),)
    return jax.shard_map(
        on_device,
        mesh=mesh,
        in_specs=placed,
        out_specs=P(("strings", "ka"), "coef", None),
        check_vma=False,
    )
```

```python
import functools

import jax
import jax.numpy as jnp
from jax import lax
from jax.experimental import pallas as pl
from jax.experimental.pallas import tpu as pltpu
from jax.sharding import PartitionSpec as P

G = 49152
NB = 384
NS_ITERS = 3
MESH = pl.DeviceIdType.MESH
MIB = 1024 * 1024
SLOTS = 4


def split(x):
    high = x.astype(jnp.bfloat16)
    low = (x - high.astype(jnp.float32)).astype(jnp.bfloat16)
    return high, low


def dot3(a, b, dims):
    a_high, a_low = split(a)
    b_high, b_low = split(b)
    dot = functools.partial(
        lax.dot_general, dimension_numbers=(dims, ((), ())), preferred_element_type=jnp.float32
    )
    return dot(a_high, b_high) + (dot(a_low, b_high) + dot(a_high, b_low))


def matmul(a, b):
    return dot3(a, b, ((1,), (0,)))


def polar(margin):
    scale = jnp.sqrt(NB * jnp.mean(margin * margin, keepdims=True) + 1e-06)
    iterate = margin / scale
    for _ in range(NS_ITERS):
        gram = matmul(iterate.T, iterate)
        iterate = 1.5 * iterate - 0.5 * matmul(iterate, gram)
    return iterate


def product_kernel(
    n, n_coef, chunks, psi_ref, product_ref,
    carried, own, part, arrived, full, unitary, theirs, pair, earlier,
    load_sem, ring_send, ring_recv, send1, recv1, send2, recv2,
    swap_send, swap_recv, hop_send, hop_recv, pass_send, pass_recv,
):
    me, my_coef = lax.axis_index("ka"), lax.axis_index("coef")
    core, chip = lax.rem(me, 2), me // 2
    pairs = n // 2
    partner = me + 1 - 2 * core
    right = lax.rem(me + 1, n)
    size = psi_ref.shape[0] // chunks
    rows = NB // n_coef
    half = NB // 2
    peers = [lax.rem(my_coef + d, n_coef) for d in range(n_coef)]

    barrier = pltpu.get_barrier_semaphore()
    for d in range(1, n):
        pl.semaphore_signal(
            barrier, inc=1, device_id={"ka": lax.rem(me + d, n)}, device_id_type=MESH
        )
    for d in range(1, n_coef):
        pl.semaphore_signal(barrier, inc=1, device_id={"coef": peers[d]}, device_id_type=MESH)
    pl.semaphore_wait(barrier, n - 1 + n_coef - 1)

    def chunk(c):
        return pl.ds(pl.multiple_of(c * size, 8), size)

    def ring(c):
        return pltpu.make_async_remote_copy(
            src_ref=psi_ref.at[chunk(c)], dst_ref=carried.at[chunk(c)],
            send_sem=ring_send.at[c], recv_sem=ring_recv.at[c],
            device_id={"ka": right}, device_id_type=MESH,
        )

    def load(c):
        slot = lax.rem(c, SLOTS)
        return pltpu.make_async_copy(psi_ref.at[chunk(c)], own.at[slot], load_sem.at[slot])

    @pl.loop(0, chunks)
    def _(c):
        ring(c).start()

    for c in range(SLOTS):
        load(c).start()
    part[...] = jnp.zeros_like(part)

    @pl.loop(0, chunks)
    def _(c):
        load(c).wait()
        ring(c).wait_recv()
        part[...] += dot3(carried[chunk(c), :], own[lax.rem(c, SLOTS)], ((0,), (0,)))

        @pl.when(c + SLOTS < chunks)
        def _():
            load(c + SLOTS).start()

    def own_rows(device):
        return pl.ds(pl.multiple_of(device * rows, 8), rows)

    def send(src, dst, send_sem, recv_sem, device):
        copy = pltpu.make_async_remote_copy(
            src_ref=src, dst_ref=dst, send_sem=send_sem, recv_sem=recv_sem,
            device_id=device, device_id_type=MESH,
        )
        copy.start()
        return copy

    scatter = [
        send(part.at[own_rows(peers[d])], arrived.at[d], send1.at[d], recv1.at[d],
             {"coef": peers[d]})
        for d in range(1, n_coef)
    ]
    total = part[own_rows(my_coef), :]
    for d in range(1, n_coef):
        scatter[d - 1].wait_recv()
        total += arrived[d]
    full[own_rows(my_coef), :] = total
    gather = [
        send(full.at[own_rows(my_coef)], full.at[own_rows(my_coef)], send2.at[d], recv2.at[d],
             {"coef": peers[d]})
        for d in range(1, n_coef)
    ]
    for copy in gather:
        copy.wait_recv()
    unitary[...] = polar(full[...] / G)

    swap = send(unitary, theirs, swap_send, swap_recv, {"ka": partner})
    swap.wait_recv()

    @pl.when(core == 0)
    def _():
        pair[...] = matmul(unitary[...], theirs[...])
        product_ref[...] = unitary[...]

    @pl.when(core == 1)
    def _():
        pair[...] = matmul(theirs[...], unitary[...])
        product_ref[...] = pair[...]

    mine = pl.ds(pl.multiple_of(core * half, 8), half)
    hops = [
        send(pair.at[mine], earlier.at[d, mine], hop_send.at[d], hop_recv.at[d],
             {"ka": 2 * lax.rem(chip + d, pairs) + core})
        for d in range(1, pairs)
    ]
    passes = []
    for d in range(1, pairs):
        hops[d - 1].wait_recv()
        passes.append(
            send(earlier.at[d, mine], earlier.at[d, mine], pass_send.at[d], pass_recv.at[d],
                 {"ka": partner})
        )
    for d in range(1, pairs):
        passes[d - 1].wait_recv()

        @pl.when(chip >= d)
        def _():
            product_ref[...] = matmul(earlier[d], product_ref[...])

    for copy in scatter + gather + [swap] + hops + passes:
        copy.wait_send()

    @pl.loop(0, chunks)
    def _(c):
        ring(c).wait_send()


def ordered_product(psi, n, n_coef, chunks):
    square = pltpu.VMEM((NB, NB), jnp.float32)
    dma = pltpu.SemaphoreType.DMA
    return pl.pallas_call(
        functools.partial(product_kernel, n, n_coef, chunks),
        out_shape=jax.ShapeDtypeStruct((NB, NB), jnp.float32),
        in_specs=[pl.BlockSpec(memory_space=pltpu.HBM)],
        out_specs=pl.BlockSpec(memory_space=pltpu.VMEM),
        scratch_shapes=[
            pltpu.VMEM(psi.shape, jnp.float32),
            pltpu.VMEM((SLOTS, psi.shape[0] // chunks, NB), jnp.float32),
            square,
            pltpu.VMEM((n_coef, NB // n_coef, NB), jnp.float32),
            square, square, square, square,
            pltpu.VMEM((n // 2, NB, NB), jnp.float32),
        ]
        + [dma((SLOTS,))]
        + [dma((chunks,))] * 2
        + [dma((n_coef,))] * 4
        + [dma] * 2
        + [dma((n // 2,))] * 4,
        compiler_params=pltpu.CompilerParams(
            collective_id=0, has_side_effects=True, vmem_limit_bytes=36 * MIB
        ),
    )(psi)


def transport_kernel(psi_ref, product_ref, out_ref, weights):
    @pl.when(pl.program_id(0) == 0)
    def _():
        high, low = split(product_ref[...].T)
        weights[...] = jnp.concatenate([high, high, low], axis=0)

    high, low = split(psi_ref[...])
    out_ref[...] = jnp.dot(
        jnp.concatenate([high, low, high], axis=1), weights[...],
        preferred_element_type=jnp.float32,
    )


def transport(psi, product):
    rows, columns = psi.shape
    block = 1024 if rows % 1024 == 0 else rows
    return pl.pallas_call(
        transport_kernel,
        grid=(rows // block,),
        out_shape=jax.ShapeDtypeStruct(psi.shape, jnp.float32),
        in_specs=[
            pl.BlockSpec((block, columns), lambda i: (i, 0)),
            pl.BlockSpec((columns, columns), lambda i: (0, 0)),
        ],
        out_specs=pl.BlockSpec((block, columns), lambda i: (i, 0)),
        scratch_shapes=[pltpu.VMEM((3 * columns, columns), jnp.bfloat16)],
        compiler_params=pltpu.CompilerParams(vmem_limit_bytes=24 * MIB),
    )(psi, product)


def on_device(wavefunctions):
    psi = wavefunctions[0]
    n_ka, n_coef = lax.axis_size("ka"), lax.axis_size("coef")
    chunks = 32
    if n_ka % 2 == 0 and NB % (8 * n_coef) == 0 and psi.shape[0] % (8 * chunks) == 0:
        return transport(psi, ordered_product(psi, n_ka, n_coef, chunks))[None]
    route = [((i - 1) % n_ka, i) for i in range(n_ka)]
    carried = lax.ppermute(psi, "ka", route)
    part = jnp.dot(carried.T, psi, precision=lax.Precision.HIGH)
    unitary = polar(lax.psum(part, "coef") / G)
    unitaries = lax.all_gather(unitary, "ka", axis=0)
    product = lax.fori_loop(
        1, lax.axis_index("ka") + 1,
        lambda k, total: jnp.dot(total, unitaries[k], precision=lax.Precision.HIGHEST),
        unitaries[0],
    )
    return transport(psi, product)[None]


def solution(mesh):
    placed = (P(("strings", "ka"), "coef", None),)
    return jax.shard_map(
        on_device,
        mesh=mesh,
        in_specs=placed,
        out_specs=P(("strings", "ka"), "coef", None),
        check_vma=False,
    )
```
